256 devices in a mesh: seq: 64 (over z, x, core), ch: 4 (over y).
Axes of the slice: x: 4, y: 4, z: 8, core: 2. Of those that a mesh axis runs over, the one named last changes fastest.
Arguments:
- layer_input: bfloat16 [16384, 4096], P('seq', 'ch'), may hold values from -6 to 6
- query_gate: bfloat16 [16384, 512], P('seq', 'ch'), may hold values from -6 to 6
- key_gate: bfloat16 [16384, 512], P('seq', 'ch'), may hold values from -6 to 6
- value_field: bfloat16 [16384, 512], P('seq', 'ch'), may hold values from -6 to 6
- out_grad: bfloat16 [16384, 512], P('seq', 'ch'), may hold values from -0.125 to 0.125
- filter_taps: float32 [16384, 512], P('seq', 'ch'), may hold values from -0.046875 to 0.046875
Outputs:
- grad_in_proj: float32 [1536, 4096], P('seq', 'ch')
- grad_filter: float32 [16384, 512], P('seq', 'ch')
The draws below stay inside these ranges and needn't reach their ends.
All inputs are finite; a program needn't handle non-finite values.
Results may differ from the reference program's by a relative error of at most 0.0029.
Values may be sent and summed in bfloat16 or wider, within the bound.
No kernel may reach another device: no remote copies, remote signals or barrier semaphores. Data moves between devices by JAX's collectives and lax.ppermute only.
A program may use at most 128 MiB of HBM per device.

```python
import jax
import jax.numpy as jnp
from jax import lax

D = 4096
C = 512
SEQ = 16384


def spiked(values, key, source, target, blocks, factor):
    owner, partner = [(jnp.arange(values.shape[position]) // (values.shape[position] // blocks)).reshape([-1 if axis == position else 1 for axis in range(values.ndim)]) for position in (source, target)]
    chosen = jax.random.permutation(key, blocks)[partner]
    strong = (owner == chosen) | (owner == (partner + blocks // 2) % blocks)
    return jnp.where(strong, factor * values, values)


def shard_levels(stream_key, dims, pieces, least, largest):
    factor_of = 1.0
    for position, parts in pieces:
        steps = jax.random.uniform(jax.random.fold_in(jax.random.fold_in(stream_key, 6), position), (parts,), jnp.float32, least / len(pieces), largest / len(pieces))
        factor_of = factor_of * jnp.repeat(jnp.exp(steps), dims[position] // parts).reshape((-1,) + (1,) * (len(dims) - 1 - position))
    return factor_of


def bell_draw(own_key, extent, scale, most, split=(), kind=jnp.bfloat16):
    factor_of = shard_levels(own_key, extent, split, -0.22, 0.18) if split else 1.0
    drawn = jax.random.normal(own_key, extent, jnp.float32) * scale * factor_of
    return jnp.minimum(jnp.maximum(drawn, -most), most).astype(kind)


def bell_draw_with(stream_key, shape, deviation, reach, pieces, heavy, kind=jnp.bfloat16):
    drawn = deviation * jax.random.normal(stream_key, shape, jnp.float32)
    if pieces:
        drawn = drawn * shard_levels(stream_key, shape, pieces, -0.22, 0.18)
    return jnp.clip(spiked(drawn, jax.random.fold_in(stream_key, 3), *heavy), -reach, reach).astype(kind)


def setup_inputs(seed: int = 0) -> dict:
    key_of = jax.random.split(jax.random.key(seed), 7)
    layer_input = bell_draw(key_of[0], (SEQ, D), 1.0, 6.0, ((0, 64), (1, 4)))
    query_gate = bell_draw(key_of[1], (SEQ, C), 1.0, 6.0, ((0, 64), (1, 4)))
    key_gate = bell_draw(key_of[2], (SEQ, C), 1.0, 6.0, ((0, 64), (1, 4)))
    value_field = bell_draw(key_of[3], (SEQ, C), 1.0, 6.0, ((0, 64), (1, 4)))
    out_grad = bell_draw_with(key_of[4], (SEQ, C), SEQ ** -0.5, 0.125, ((0, 64), (1, 4)), (0, 1, 64, 4.0))
    filter_taps = bell_draw(key_of[5], (SEQ, C), SEQ ** -0.5, 0.046875, ((0, 64), (1, 4)), jnp.float32)
    return {"layer_input": layer_input, "query_gate": query_gate, "key_gate": key_gate, "value_field": value_field, "out_grad": out_grad, "filter_taps": filter_taps}


def convolve_block(fields):
    gated_field, upstream, taps = fields
    length = gated_field.shape[0]
    gated_spec = jnp.fft.rfft(gated_field, n=2 * length, axis=0)
    upstream_spec = jnp.fft.rfft(upstream, n=2 * length, axis=0)
    taps_spec = jnp.fft.rfft(taps, n=2 * length, axis=0)
    conv_out = jnp.fft.irfft(taps_spec * gated_spec, n=2 * length, axis=0)[:length]
    gated_grad = jnp.fft.irfft(jnp.conj(taps_spec) * upstream_spec, n=2 * length, axis=0)[:length]
    lag_grad = jnp.fft.irfft(jnp.conj(gated_spec) * upstream_spec, n=2 * length, axis=0)[:length]
    return (conv_out.astype(gated_field.dtype), gated_grad.astype(gated_field.dtype), lag_grad.astype(gated_field.dtype))


def reference(layer_input, query_gate, key_gate, value_field, out_grad, filter_taps):
    gated_field = key_gate.astype(jnp.float32) * value_field.astype(jnp.float32)
    upstream = out_grad.astype(jnp.float32) * query_gate.astype(jnp.float32)
    length, channels = gated_field.shape
    block_width = min(channels, 64)
    block_count = channels // block_width

    def to_blocks(source):
        return source.reshape(length, block_count, block_width).transpose(1, 0, 2)

    def from_blocks(source):
        return source.transpose(1, 0, 2).reshape(length, channels)

    conv_out, gated_grad, lag_grad = lax.map(convolve_block, (to_blocks(gated_field), to_blocks(upstream), to_blocks(filter_taps.astype(jnp.float32))))
    conv_out = from_blocks(conv_out)
    gated_grad = from_blocks(gated_grad)
    grad_filter = from_blocks(lag_grad)
    grad_query = (out_grad.astype(jnp.float32) * conv_out).astype(jnp.bfloat16)
    grad_key = (gated_grad * value_field.astype(jnp.float32)).astype(jnp.bfloat16)
    grad_value = (gated_grad * key_gate.astype(jnp.float32)).astype(jnp.bfloat16)
    stacked = jnp.concatenate([grad_query, grad_key, grad_value], axis=1)
    grad_in_proj = lax.dot_general(stacked, layer_input, (((0,), (0,)), ((), ())), preferred_element_type=jnp.float32)
    return grad_in_proj, grad_filter
```

```python
import jax
import jax.numpy as jnp
import numpy as np
from jax import lax
from jax.experimental import pallas as pl
from jax.experimental.pallas import tpu as pltpu
from jax.sharding import Mesh
from jax.sharding import PartitionSpec as P

NZ, NX, NCORE, NP, NY = 8, 4, 2, 8, 4
BLOCKS, BLOCK_LEN, SHARD_CH = 64, 256, 128
BINS, TRANSFORM = 64, 32768
bf16, f32 = jnp.bfloat16, jnp.float32


def split_np(table):
    high = table.astype(np.float32).astype(jnp.bfloat16)
    low = (table - high.astype(np.float64)).astype(jnp.bfloat16)
    return high, low


def pack_order():
    order = np.zeros((8 * BLOCKS, 4 * SHARD_CH), np.float32)
    for z in range(NZ):
        for p in range(NP):
            for s in range(2):
                for j in range(2):
                    for half in range(2):
                        row = (8 * z + p) * 8 + 4 * s + 2 * j + half
                        order[row, (2 * s + half) * SHARD_CH + 64 * j + 8 * p + z] = 1.0
    return order.astype(jnp.bfloat16)


def tables():
    bins = np.arange(BINS, dtype=np.float64) + 0.5
    held = np.array([8 * z + p for p in range(NP) for z in range(NZ)], np.float64)
    lag = np.arange(BLOCK_LEN, dtype=np.float64)
    first = 2.0 * np.pi / 128.0 * bins[:, None] * held[None, :]
    twist = 2.0 * np.pi / TRANSFORM * bins[:, None] * lag[None, :]
    second = 2.0 * np.pi / BLOCK_LEN * ((lag[:, None] * lag[None, :]) % BLOCK_LEN)
    ahead_high, ahead_low = split_np(np.concatenate([np.cos(first), -np.sin(first)], axis=0))
    ahead = np.concatenate([ahead_high, ahead_high, ahead_low], axis=1)
    back = np.concatenate([np.cos(first).T, -np.sin(first).T], axis=1) * (2.0 / TRANSFORM)
    back_high, back_low = split_np(back)
    back = np.concatenate([back_high, back_high, back_low], axis=1)
    cosine, sine = np.cos(second), np.sin(second)
    outer_high, outer_low = split_np(np.block([[cosine, -sine], [sine, cosine]]))
    turn = np.stack([np.cos(twist), -np.sin(twist)]).astype(np.float32)
    return ahead, back, turn, outer_high, outer_low


def split(value):
    high = value.astype(bf16)
    low = (value - high.astype(f32)).astype(bf16)
    return high, low


def product(left, right, dims):
    return lax.dot_general(left, right, (dims, ((), ())), preferred_element_type=f32)


def pack_kernel(key_ref, value_ref, grad_ref, query_ref, taps_ref, order_ref, out_ref):
    taps_high, taps_low = split(taps_ref[...])
    order = order_ref[...]

    def tile(first, second):
        wide = jnp.concatenate(
            [first[:128], first[128:], second[:128], second[128:]], axis=1
        )
        return product(order, wide, ((1,), (1,))).reshape(BLOCKS, 8, 128)

    out_ref[...] = jnp.concatenate(
        [
            tile(key_ref[...], value_ref[...]),
            tile(grad_ref[...], query_ref[...]),
            tile(taps_high, taps_low),
        ],
        axis=1,
    ).astype(bf16)


def conv_kernel(
    got_ref, ahead_ref, back_ref, turn_ref, high_ref, low_ref, out_ref, lag_ref, rows_ref, lag_rows_ref
):
    rows_ref[...] = got_ref[...].astype(f32).reshape(BLOCKS * 24, 128)

    def field(number):
        parts = []
        for p in range(NP):
            parts.append(
                jnp.concatenate(
                    [rows_ref[pl.ds(p * 24 + number * 4 + r, 8, stride=192), :] for r in range(4)],
                    axis=1,
                )
            )
        return jnp.concatenate(parts, axis=0)

    key, value, grad, query = field(0), field(1), field(2), field(3)
    taps = field(4) + field(5)
    signals = jnp.concatenate([taps, key * value, grad * query], axis=1)
    sig_high, sig_low = split(signals)
    mixed = product(
        ahead_ref[...], jnp.concatenate([sig_high, sig_low, sig_high], axis=0), ((1,), (0,))
    )
    turn_real, turn_imag = turn_ref[0], turn_ref[1]
    turned = []
    for block in range(6):
        real = mixed[:BINS, 256 * block : 256 * (block + 1)]
        imag = mixed[BINS:, 256 * block : 256 * (block + 1)]
        turned.append(
            jnp.concatenate(
                [real * turn_real - imag * turn_imag, real * turn_imag + imag * turn_real], axis=1
            )
        )
    outer_high, outer_low = high_ref[...], low_ref[...]

    def outer(source, dims):
        high, low = split(source)
        return (
            product(high, outer_high, dims)
            + product(low, outer_high, dims)
            + product(high, outer_low, dims)
        )

    spec = outer(jnp.concatenate(turned, axis=0), ((1,), (0,)))
    tr, ti = spec[:128, :256], spec[:128, 256:]
    vr, vi = spec[128:256, :256], spec[128:256, 256:]
    ur, ui = spec[256:, :256], spec[256:, 256:]
    mixes = jnp.concatenate(
        [
            jnp.concatenate([tr * vr - ti * vi, tr * vi + ti * vr], axis=1),
            jnp.concatenate([tr * ur + ti * ui, tr * ui - ti * ur], axis=1),
            jnp.concatenate([vr * ur + vi * ui, vr * ui - vi * ur], axis=1),
        ],
        axis=0,
    )
    home = outer(mixes, ((1,), (1,)))
    reals, imags = [], []
    for block in range(6):
        real = home[BINS * block : BINS * (block + 1), :256]
        imag = home[BINS * block : BINS * (block + 1), 256:]
        reals.append(real * turn_real + imag * turn_imag)
        imags.append(imag * turn_real - real * turn_imag)
    untwisted = jnp.concatenate(
        [jnp.concatenate(reals, axis=1), jnp.concatenate(imags, axis=1)], axis=0
    )
    home_high, home_low = split(untwisted)
    result = product(
        back_ref[...], jnp.concatenate([home_high, home_low, home_high], axis=0), ((1,), (0,))
    )
    conv_out, gated_grad, lag_grad = result[:, :512], result[:, 512:1024], result[:, 1024:]
    stacked = (grad * conv_out, gated_grad * value, gated_grad * key)
    for p in range(NP):
        block = jnp.concatenate(
            [
                field_rows[8 * p : 8 * p + 8, 128 * lane : 128 * lane + 128]
                for field_rows in stacked
                for lane in range(4)
            ],
            axis=0,
        ).astype(bf16)
        for y in range(NY):
            out_ref[p * NY + y] = block
    lag_high = lag_grad.astype(bf16).astype(f32)
    lag_low = lag_grad - lag_high
    for level, part in ((0, lag_high), (1, lag_low)):
        for p in range(NP):
            for r in range(4):
                lag_rows_ref[pl.ds(p * 8 + 4 * level + r, 8, stride=64), :] = part[
                    8 * p : 8 * p + 8, 128 * r : 128 * r + 128
                ]
    lag_ref[...] = lag_rows_ref[...].reshape(BLOCKS, 8, 128)


def share_kernel(got_ref, input_ref, lag_ref, out_ref, rows_ref, held_ref, sums_ref, done):
    copy = pltpu.make_async_copy(input_ref, held_ref, done)
    copy.start()
    rows_ref[...] = got_ref[...].astype(f32).reshape(32 * 96, 128)
    left = []
    for z in range(NZ):
        tiles = []
        for kind in range(3):
            for y in range(NY):
                for j in range(2):
                    lane = kind * 4 + j * 2
                    tiles.append(
                        jnp.concatenate(
                            [
                                rows_ref[pl.ds(y * 96 + (lane + half) * 8 + z, 8, stride=384), :]
                                for half in range(2)
                            ],
                            axis=1,
                        )
                    )
        left.append(jnp.concatenate(tiles, axis=0).astype(bf16))
    left = jnp.concatenate(left, axis=1)
    copy.wait()
    total = product(left, held_ref[...], ((1,), (0,)))
    for lane in range(8):
        sums_ref[pl.ds(lane, 192, stride=8), :] = total[:, 128 * lane : 128 * lane + 128]
    out_ref[...] = jnp.concatenate(
        [sums_ref[...].reshape(BLOCKS, 24, 128), lag_ref[...]], axis=1
    ).astype(bf16)


def finish_kernel(got_ref, proj_ref, filter_ref, sums_ref, rows_ref):
    wide = got_ref[...].astype(f32)
    sums_ref[...] = (
        wide.reshape(NZ, NP, 32, 128)[:, :, :24, :].sum(axis=1).reshape(NZ * 24, 128)
    )
    for e in range(3):
        for lane in range(8):
            proj_ref[8 * e : 8 * e + 8, 128 * lane : 128 * lane + 128] = sums_ref[
                pl.ds(8 * e + lane, 8, stride=24), :
            ]
    rows_ref[...] = wide.reshape(BLOCKS * 32, 128)
    for half in range(2):
        tiles = []
        for j in range(2):
            for p in range(NP):
                start = p * 32 + 24 + 2 * j + half
                tiles.append(
                    rows_ref[pl.ds(start, 8, stride=256), :]
                    + rows_ref[pl.ds(start + 4, 8, stride=256), :]
                )
        filter_ref[128 * half : 128 * half + 128, :] = jnp.concatenate(tiles, axis=0).T


VMEM = pltpu.VMEM


def call(kernel, name, args, outs, scratch, spaces=None):
    spaces = spaces or [pltpu.VMEM] * len(args)
    return pl.pallas_call(
        kernel,
        out_shape=outs,
        in_specs=[pl.BlockSpec(memory_space=space) for space in spaces],
        out_specs=jax.tree.map(lambda _: pl.BlockSpec(memory_space=pltpu.VMEM), outs),
        scratch_shapes=scratch,
        compiler_params=pltpu.CompilerParams(vmem_limit_bytes=48 * 2**20),
        name=name,
    )(*args)


def on_device(layer_input, query_gate, key_gate, value_field, out_grad, filter_taps):
    held_input = lax.all_gather(layer_input, "z", axis=0, tiled=True)
    ahead, back, turn, outer_high, outer_low = (jnp.asarray(t) for t in tables())
    packed = call(
        pack_kernel,
        "pack",
        (key_gate, value_field, out_grad, query_gate, filter_taps, jnp.asarray(pack_order())),
        jax.ShapeDtypeStruct((BLOCKS, 24, 128), bf16),
        [],
    )
    fields = lax.all_to_all(packed, ("z", "x", "core"), split_axis=0, concat_axis=0, tiled=True)
    grads, lags = call(
        conv_kernel,
        "conv",
        (fields, ahead, back, turn, outer_high, outer_low),
        (
            jax.ShapeDtypeStruct((NP * NY, 96, 128), bf16),
            jax.ShapeDtypeStruct((BLOCKS, 8, 128), f32),
        ),
        [VMEM((BLOCKS * 24, 128), f32), VMEM((BLOCKS * 8, 128), f32)],
    )
    stacked = lax.all_to_all(grads, ("x", "core", "y"), split_axis=0, concat_axis=0, tiled=True)
    shares = call(
        share_kernel,
        "share",
        (stacked, held_input, lags),
        jax.ShapeDtypeStruct((BLOCKS, 32, 128), bf16),
        [
            VMEM((32 * 96, 128), f32),
            VMEM((2048, 1024), bf16),
            VMEM((1536, 128), f32),
            pltpu.SemaphoreType.DMA,
        ],
        [pltpu.VMEM, pl.ANY, pltpu.VMEM],
    )
    parts = lax.all_to_all(shares, ("z", "x", "core"), split_axis=0, concat_axis=0, tiled=True)
    return call(
        finish_kernel,
        "finish",
        (parts,),
        (
            jax.ShapeDtypeStruct((24, 1024), f32),
            jax.ShapeDtypeStruct((BLOCK_LEN, SHARD_CH), f32),
        ),
        [VMEM((NZ * 24, 128), f32), VMEM((BLOCKS * 32, 128), f32)],
    )


def solution(mesh):
    fine = Mesh(mesh.devices.reshape(NZ, NX, NCORE, NY), ("z", "x", "core", "y"))
    spec = P(("z", "x", "core"), "y")
    return jax.shard_map(
        on_device,
        mesh=fine,
        in_specs=(spec,) * 6,
        out_specs=(spec, spec),
        check_vma=False,
    )
```

```python
import jax
import jax.numpy as jnp
import numpy as np
from jax import lax
from jax.experimental import pallas as pl
from jax.experimental.pallas import tpu as pltpu
from jax.sharding import Mesh
from jax.sharding import PartitionSpec as P

NZ, NX, NCORE, NA, NY = 8, 4, 2, 8, 4
BLOCKS, BLOCK_LEN, SHARD_CH = 64, 256, 128
BINS, TRANSFORM = 64, 32768
bf16, f32 = jnp.bfloat16, jnp.float32


def split_np(table):
    high = table.astype(np.float32).astype(jnp.bfloat16)
    low = (table - high.astype(np.float64)).astype(jnp.bfloat16)
    return high, low


def pack_order():
    order = np.zeros((8 * BLOCKS, 4 * SHARD_CH), np.float32)
    for i in range(BLOCKS):
        for s in range(2):
            for j in range(2):
                for half in range(2):
                    row = i * 8 + 4 * s + 2 * j + half
                    order[row, (2 * s + half) * SHARD_CH + 64 * j + i] = 1.0
    return order.astype(jnp.bfloat16)


def tables():
    bins = np.arange(BINS, dtype=np.float64) + 0.5
    held = np.arange(BLOCKS, dtype=np.float64)
    lag = np.arange(BLOCK_LEN, dtype=np.float64)
    first = 2.0 * np.pi / 128.0 * bins[:, None] * held[None, :]
    twist = 2.0 * np.pi / TRANSFORM * bins[:, None] * lag[None, :]
    second = 2.0 * np.pi / BLOCK_LEN * ((lag[:, None] * lag[None, :]) % BLOCK_LEN)
    ahead_high, ahead_low = split_np(np.concatenate([np.cos(first), -np.sin(first)], axis=0))
    back = np.concatenate([np.cos(first).T, -np.sin(first).T], axis=1) * (2.0 / TRANSFORM)
    back_high, back_low = split_np(back)
    cosine, sine = np.cos(second), np.sin(second)
    outer = split_np(np.block([[cosine, -sine], [sine, cosine]]))
    turn = split_np(np.concatenate([np.cos(twist), -np.sin(twist)], axis=1))
    ahead = np.concatenate([ahead_high, ahead_high, ahead_low], axis=1)
    back = np.concatenate([back_high, back_high, back_low], axis=1)
    ahead = np.pad(ahead, ((0, 0), (0, 512 - ahead.shape[1])))
    back = np.pad(back, ((0, 0), (0, 512 - back.shape[1])))
    return np.concatenate([*outer, *turn, ahead, back], axis=0)


def split(value):
    high = value.astype(bf16)
    low = (value - high.astype(f32)).astype(bf16)
    return high, low


def product(left, right, dims):
    return lax.dot_general(left, right, (dims, ((), ())), preferred_element_type=f32)


def fetch(pairs, done):
    copies = [
        pltpu.make_async_copy(source, target, done.at[number])
        for number, (source, target) in enumerate(pairs)
    ]
    for copy in copies:
        copy.start()
    return copies


def pack_kernel(key_in, value_in, grad_in, query_in, taps_in, order_in, out_ref, *scratch):
    *held, done = scratch
    key_ref, value_ref, grad_ref, query_ref, taps_ref, order_ref = held
    sources = (key_in, value_in, grad_in, query_in, taps_in, order_in)
    for copy in fetch(zip(sources, held, strict=True), done):
        copy.wait()
    taps_high, taps_low = split(taps_ref[...])
    order = order_ref[...]

    def tile(first, second):
        wide = jnp.concatenate(
            [first[:128], first[128:], second[:128], second[128:]], axis=1
        )
        return product(order, wide, ((1,), (1,))).reshape(BLOCKS, 8, 128)

    out_ref[...] = jnp.concatenate(
        [
            tile(key_ref[...], value_ref[...]),
            tile(grad_ref[...], query_ref[...]),
            tile(taps_high, taps_low),
        ],
        axis=1,
    ).astype(bf16)


def conv_kernel(got_ref, table_ref, out_ref, lag_ref, rows_ref, lag_rows_ref):
    rows_ref[...] = got_ref[...].astype(f32).reshape(BLOCKS * 24, 128)

    def field(number):
        parts = []
        for z in range(NZ):
            parts.append(
                jnp.concatenate(
                    [rows_ref[pl.ds(z * 192 + number * 4 + r, 8, stride=24), :] for r in range(4)],
                    axis=1,
                )
            )
        return jnp.concatenate(parts, axis=0)

    key, value, grad, query = field(0), field(1), field(2), field(3)
    taps = field(4) + field(5)
    signals = jnp.concatenate([taps, key * value, grad * query], axis=1)
    sig_high, sig_low = split(signals)
    mixed = product(
        table_ref[1152:1280, :192], jnp.concatenate([sig_high, sig_low, sig_high], axis=0), ((1,), (0,))
    )
    turn = table_ref[1024:1088].astype(f32) + table_ref[1088:1152].astype(f32)
    turn_real, turn_imag = turn[:, :256], turn[:, 256:]
    turned = []
    for block in range(6):
        real = mixed[:BINS, 256 * block : 256 * (block + 1)]
        imag = mixed[BINS:, 256 * block : 256 * (block + 1)]
        turned.append(
            jnp.concatenate(
                [real * turn_real - imag * turn_imag, real * turn_imag + imag * turn_real], axis=1
            )
        )
    outer_high, outer_low = table_ref[:512], table_ref[512:1024]

    def outer(source, dims):
        high, low = split(source)
        return (
            product(high, outer_high, dims)
            + product(low, outer_high, dims)
            + product(high, outer_low, dims)
        )

    spec = outer(jnp.concatenate(turned, axis=0), ((1,), (0,)))
    tr, ti = spec[:128, :256], spec[:128, 256:]
    vr, vi = spec[128:256, :256], spec[128:256, 256:]
    ur, ui = spec[256:, :256], spec[256:, 256:]
    mixes = jnp.concatenate(
        [
            jnp.concatenate([tr * vr - ti * vi, tr * vi + ti * vr], axis=1),
            jnp.concatenate([tr * ur + ti * ui, tr * ui - ti * ur], axis=1),
            jnp.concatenate([vr * ur + vi * ui, vr * ui - vi * ur], axis=1),
        ],
        axis=0,
    )
    home = outer(mixes, ((1,), (1,)))
    reals, imags = [], []
    for block in range(6):
        real = home[BINS * block : BINS * (block + 1), :256]
        imag = home[BINS * block : BINS * (block + 1), 256:]
        reals.append(real * turn_real + imag * turn_imag)
        imags.append(imag * turn_real - real * turn_imag)
    untwisted = jnp.concatenate(
        [jnp.concatenate(reals, axis=1), jnp.concatenate(imags, axis=1)], axis=0
    )
    home_high, home_low = split(untwisted)
    result = product(
        table_ref[1280:1344, :384], jnp.concatenate([home_high, home_low, home_high], axis=0), ((1,), (0,))
    )
    conv_out, gated_grad, lag_grad = result[:, :512], result[:, 512:1024], result[:, 1024:]
    stacked = (grad * conv_out, gated_grad * value, gated_grad * key)
    for z in range(NZ):
        block = jnp.concatenate(
            [
                field_rows[8 * z : 8 * z + 8, 128 * lane : 128 * lane + 128]
                for field_rows in stacked
                for lane in range(4)
            ],
            axis=0,
        ).astype(bf16)
        for y in range(NY):
            out_ref[z * NY + y] = block
    lag_high = lag_grad.astype(bf16).astype(f32)
    lag_low = lag_grad - lag_high
    for level, part in ((0, lag_high), (1, lag_low)):
        for z in range(NZ):
            for r in range(4):
                lag_rows_ref[pl.ds(z * 64 + 4 * level + r, 8, stride=8), :] = part[
                    8 * z : 8 * z + 8, 128 * r : 128 * r + 128
                ]
    lag_ref[...] = lag_rows_ref[...].reshape(BLOCKS, 8, 128)


def share_kernel(got_ref, lag_ref, *rest):
    inputs, (out_ref, rows_ref, held_ref, sums_ref, done) = rest[:14], rest[14:]
    x, core = lax.axis_index("x"), lax.axis_index("core")
    across = lax.rem(x + 2, NX)
    beside = x + 1 - 2 * lax.rem(x, 2)
    half = BLOCK_LEN // 2
    pairs = []
    for swap, unit in ((0, core), (1, 1 - core)):
        for source, (place, offset, length) in zip(
            inputs[7 * swap : 7 * swap + 7],
            (
                (x, 0, BLOCK_LEN),
                (beside, half, half),
                (NX - 1 - x, 0, half),
                (beside, 0, half),
                (NX - 1 - x, half, half),
                (across, 0, half),
                (across, half, half),
            ),
            strict=True,
        ):
            start = pl.multiple_of((NCORE * place + unit) * BLOCK_LEN + offset, half)
            pairs.append((source, held_ref.at[pl.ds(start, length)]))
    copies = fetch(pairs, done)
    rows_ref[...] = got_ref[...].astype(f32).reshape(32 * 96, 128)
    left = []
    for a in range(NA):
        tiles = []
        for kind in range(3):
            for y in range(NY):
                for j in range(2):
                    lane = kind * 4 + j * 2
                    tiles.append(
                        jnp.concatenate(
                            [
                                rows_ref[pl.ds(y * 96 + (lane + half) * 8 + a, 8, stride=384), :]
                                for half in range(2)
                            ],
                            axis=1,
                        )
                    )
        left.append(jnp.concatenate(tiles, axis=0).astype(bf16))
    left = jnp.concatenate(left, axis=1)
    for copy in copies:
        copy.wait()
    total = product(left, held_ref[...], ((1,), (0,)))
    for lane in range(8):
        sums_ref[pl.ds(lane, 192, stride=8), :] = total[:, 128 * lane : 128 * lane + 128]
    out_ref[...] = jnp.concatenate(
        [sums_ref[...].reshape(BLOCKS, 24, 128), lag_ref[...]], axis=1
    ).astype(bf16)


def finish_kernel(got_ref, proj_ref, filter_ref, sums_ref, rows_ref):
    wide = got_ref[...].astype(f32)
    sums_ref[...] = (
        wide.reshape(NZ, NA, 32, 128)[:, :, :24, :].sum(axis=0).reshape(NA * 24, 128)
    )
    for e in range(3):
        for lane in range(8):
            proj_ref[8 * e : 8 * e + 8, 128 * lane : 128 * lane + 128] = sums_ref[
                pl.ds(8 * e + lane, 8, stride=24), :
            ]
    rows_ref[...] = wide.reshape(BLOCKS * 32, 128)
    for half in range(2):
        tiles = []
        for j in range(2):
            for z in range(NZ):
                start = z * 256 + 24 + 2 * j + half
                tiles.append(
                    rows_ref[pl.ds(start, 8, stride=32), :]
                    + rows_ref[pl.ds(start + 4, 8, stride=32), :]
                )
        filter_ref[128 * half : 128 * half + 128, :] = jnp.concatenate(tiles, axis=0).T


VMEM, HBM = pltpu.VMEM, pltpu.HBM


def call(kernel, name, args, spaces, outs, scratch, grant):
    return pl.pallas_call(
        kernel,
        out_shape=outs,
        in_specs=[pl.BlockSpec(memory_space=space) for space in spaces],
        out_specs=jax.tree.map(lambda _: pl.BlockSpec(memory_space=VMEM), outs),
        scratch_shapes=scratch,
        compiler_params=pltpu.CompilerParams(vmem_limit_bytes=grant * 2**20),
        name=name,
    )(*args)


def held_like(arrays):
    return [VMEM(array.shape, array.dtype) for array in arrays] + [
        pltpu.SemaphoreType.DMA((len(arrays),))
    ]


def on_device(layer_input, query_gate, key_gate, value_field, out_grad, filter_taps):
    pairs, rings = [(0, 1), (1, 0), (2, 3), (3, 2)], [(0, 3), (3, 0), (1, 2), (2, 1)]
    half = BLOCK_LEN // 2
    near_low = lax.ppermute(layer_input[half:], "x", pairs)
    far_high = lax.ppermute(layer_input[:half], "x", rings)
    sources = (key_gate, value_field, out_grad, query_gate, filter_taps, jnp.asarray(pack_order()))
    packed = call(
        pack_kernel,
        "pack",
        sources,
        [HBM] * 6,
        jax.ShapeDtypeStruct((BLOCKS, 24, 128), bf16),
        held_like(sources),
        60,
    )
    fields = lax.all_to_all(packed, ("z", "x", "core"), split_axis=0, concat_axis=0, tiled=True)
    grads, lags = call(
        conv_kernel,
        "conv",
        (fields, jnp.asarray(tables())),
        [VMEM] * 2,
        (
            jax.ShapeDtypeStruct((NZ * NY, 96, 128), bf16),
            jax.ShapeDtypeStruct((BLOCKS, 8, 128), f32),
        ),
        [VMEM((BLOCKS * 24, 128), f32), VMEM((BLOCKS * 8, 128), f32)],
        32,
    )
    grads, held, near_low, far_high = lax.optimization_barrier(
        (grads, layer_input, near_low, far_high)
    )
    near_high = lax.ppermute(held[:half], "x", pairs)
    far_low = lax.ppermute(held[half:], "x", rings)
    across_high = lax.ppermute(far_high, "x", pairs)
    across_low = lax.ppermute(near_low, "x", rings)
    own = (layer_input, near_low, far_high, near_high, far_low, across_high, across_low)
    other = [lax.ppermute(block, "core", [(0, 1), (1, 0)]) for block in own]
    stacked = lax.all_to_all(grads, ("z", "y"), split_axis=0, concat_axis=0, tiled=True)
    shares = call(
        share_kernel,
        "share",
        (stacked, lags, *own, *other),
        [VMEM, VMEM] + [pl.ANY] * 14,
        jax.ShapeDtypeStruct((BLOCKS, 32, 128), bf16),
        [
            VMEM((32 * 96, 128), f32),
            VMEM((2048, 1024), bf16),
            VMEM((1536, 128), f32),
            pltpu.SemaphoreType.DMA((14,)),
        ],
        52,
    )
    parts = lax.all_to_all(shares, ("z", "x", "core"), split_axis=0, concat_axis=0, tiled=True)
    return call(
        finish_kernel,
        "finish",
        (parts,),
        [VMEM],
        (
            jax.ShapeDtypeStruct((24, 1024), f32),
            jax.ShapeDtypeStruct((BLOCK_LEN, SHARD_CH), f32),
        ),
        [VMEM((NA * 24, 128), f32), VMEM((BLOCKS * 32, 128), f32)],
        32,
    )


def solution(mesh):
    fine = Mesh(mesh.devices.reshape(NZ, NX, NCORE, NY), ("z", "x", "core", "y"))
    spec = P(("z", "x", "core"), "y")
    return jax.shard_map(
        on_device,
        mesh=fine,
        in_specs=(spec,) * 6,
        out_specs=(spec, spec),
        check_vma=False,
    )
```

```python
import jax
import jax.numpy as jnp
import numpy as np
from jax import lax
from jax.experimental import pallas as pl
from jax.experimental.pallas import tpu as pltpu
from jax.sharding import Mesh
from jax.sharding import PartitionSpec as P

NZ, NX, NCORE, NA, NY = 8, 4, 2, 8, 4
BLOCKS, BLOCK_LEN, SHARD_CH = 64, 256, 128
BINS, TRANSFORM = 64, 32768
bf16, f32 = jnp.bfloat16, jnp.float32


def split_np(table):
    high = table.astype(np.float32).astype(jnp.bfloat16)
    low = (table - high.astype(np.float64)).astype(jnp.bfloat16)
    return high, low


def pack_order():
    order = np.zeros((8 * BLOCKS, 4 * SHARD_CH), np.float32)
    for i in range(BLOCKS):
        for s in range(2):
            for j in range(2):
                for half in range(2):
                    row = i * 8 + 4 * s + 2 * j + half
                    order[row, (2 * s + half) * SHARD_CH + 64 * j + i] = 1.0
    return order.astype(jnp.bfloat16)


def tables():
    bins = np.arange(BINS, dtype=np.float64) + 0.5
    held = np.arange(BLOCKS, dtype=np.float64)
    lag = np.arange(BLOCK_LEN, dtype=np.float64)
    first = 2.0 * np.pi / 128.0 * bins[:, None] * held[None, :]
    twist = 2.0 * np.pi / TRANSFORM * bins[:, None] * lag[None, :]
    second = 2.0 * np.pi / BLOCK_LEN * ((lag[:, None] * lag[None, :]) % BLOCK_LEN)
    ahead_high, ahead_low = split_np(np.concatenate([np.cos(first), -np.sin(first)], axis=0))
    back = np.concatenate([np.cos(first).T, -np.sin(first).T], axis=1) * (2.0 / TRANSFORM)
    back_high, back_low = split_np(back)
    cosine, sine = np.cos(second), np.sin(second)
    outer = split_np(np.block([[cosine, -sine], [sine, cosine]]))
    turn = split_np(np.concatenate([np.cos(twist), -np.sin(twist)], axis=1))
    ahead = np.concatenate([ahead_high, ahead_high, ahead_low], axis=1)
    back = np.concatenate([back_high, back_high, back_low], axis=1)
    ahead = np.pad(ahead, ((0, 0), (0, 512 - ahead.shape[1])))
    back = np.pad(back, ((0, 0), (0, 512 - back.shape[1])))
    return np.concatenate([*outer, *turn, ahead, back], axis=0)


def split(value):
    high = value.astype(bf16)
    low = (value - high.astype(f32)).astype(bf16)
    return high, low


def product(left, right, dims):
    return lax.dot_general(left, right, (dims, ((), ())), preferred_element_type=f32)


def fetch(pairs, done):
    copies = [
        pltpu.make_async_copy(source, target, done.at[number])
        for number, (source, target) in enumerate(pairs)
    ]
    for copy in copies:
        copy.start()
    return copies


def pack_kernel(key_in, value_in, grad_in, query_in, taps_in, order_in, out_ref, *scratch):
    *held, done = scratch
    key_ref, value_ref, grad_ref, query_ref, taps_ref, order_ref = held
    sources = (key_in, value_in, grad_in, query_in, taps_in, order_in)
    for copy in fetch(zip(sources, held, strict=True), done):
        copy.wait()
    taps_high, taps_low = split(taps_ref[...])
    order = order_ref[...]

    def tile(first, second):
        wide = jnp.concatenate(
            [first[:128], first[128:], second[:128], second[128:]], axis=1
        )
        return product(order, wide, ((1,), (1,))).reshape(BLOCKS, 8, 128)

    out_ref[...] = jnp.concatenate(
        [
            tile(key_ref[...], value_ref[...]),
            tile(grad_ref[...], query_ref[...]),
            tile(taps_high, taps_low),
        ],
        axis=1,
    ).astype(bf16)


def conv_kernel(got_ref, table_ref, out_ref, lag_ref, rows_ref, lag_rows_ref):
    rows_ref[...] = got_ref[...].astype(f32).reshape(BLOCKS * 24, 128)

    def field(number):
        parts = []
        for z in range(NZ):
            parts.append(
                jnp.concatenate(
                    [rows_ref[pl.ds(z * 192 + number * 4 + r, 8, stride=24), :] for r in range(4)],
                    axis=1,
                )
            )
        return jnp.concatenate(parts, axis=0)

    key, value, grad, query = field(0), field(1), field(2), field(3)
    taps = field(4) + field(5)
    signals = jnp.concatenate([taps, key * value, grad * query], axis=1)
    sig_high, sig_low = split(signals)
    mixed = product(
        table_ref[1152:1280, :192], jnp.concatenate([sig_high, sig_low, sig_high], axis=0), ((1,), (0,))
    )
    turn = table_ref[1024:1088].astype(f32) + table_ref[1088:1152].astype(f32)
    turn_real, turn_imag = turn[:, :256], turn[:, 256:]
    turned = []
    for block in range(6):
        real = mixed[:BINS, 256 * block : 256 * (block + 1)]
        imag = mixed[BINS:, 256 * block : 256 * (block + 1)]
        turned.append(
            jnp.concatenate(
                [real * turn_real - imag * turn_imag, real * turn_imag + imag * turn_real], axis=1
            )
        )
    outer_high, outer_low = table_ref[:512], table_ref[512:1024]

    def outer(source, dims):
        high, low = split(source)
        return (
            product(high, outer_high, dims)
            + product(low, outer_high, dims)
            + product(high, outer_low, dims)
        )

    spec = outer(jnp.concatenate(turned, axis=0), ((1,), (0,)))
    tr, ti = spec[:128, :256], spec[:128, 256:]
    vr, vi = spec[128:256, :256], spec[128:256, 256:]
    ur, ui = spec[256:, :256], spec[256:, 256:]
    mixes = jnp.concatenate(
        [
            jnp.concatenate([tr * vr - ti * vi, tr * vi + ti * vr], axis=1),
            jnp.concatenate([tr * ur + ti * ui, tr * ui - ti * ur], axis=1),
            jnp.concatenate([vr * ur + vi * ui, vr * ui - vi * ur], axis=1),
        ],
        axis=0,
    )
    home = outer(mixes, ((1,), (1,)))
    reals, imags = [], []
    for block in range(6):
        real = home[BINS * block : BINS * (block + 1), :256]
        imag = home[BINS * block : BINS * (block + 1), 256:]
        reals.append(real * turn_real + imag * turn_imag)
        imags.append(imag * turn_real - real * turn_imag)
    untwisted = jnp.concatenate(
        [jnp.concatenate(reals, axis=1), jnp.concatenate(imags, axis=1)], axis=0
    )
    home_high, home_low = split(untwisted)
    result = product(
        table_ref[1280:1344, :384], jnp.concatenate([home_high, home_low, home_high], axis=0), ((1,), (0,))
    )
    conv_out, gated_grad, lag_grad = result[:, :512], result[:, 512:1024], result[:, 1024:]
    stacked = (grad * conv_out, gated_grad * value, gated_grad * key)
    for z in range(NZ):
        block = jnp.concatenate(
            [
                field_rows[8 * z : 8 * z + 8, 128 * lane : 128 * lane + 128]
                for field_rows in stacked
                for lane in range(4)
            ],
            axis=0,
        ).astype(bf16)
        for y in range(NY):
            out_ref[z * NY + y] = block
    lag_high = lag_grad.astype(bf16).astype(f32)
    lag_low = lag_grad - lag_high
    for level, part in ((0, lag_high), (1, lag_low)):
        for z in range(NZ):
            for r in range(4):
                lag_rows_ref[pl.ds(z * 64 + 4 * level + r, 8, stride=8), :] = part[
                    8 * z : 8 * z + 8, 128 * r : 128 * r + 128
                ]
    lag_ref[...] = lag_rows_ref[...].reshape(BLOCKS, 8, 128)


def share_kernel(got_in, lag_in, *rest):
    inputs, (out_ref, got_ref, lag_ref, rows_ref, held_ref, sums_ref, done) = rest[:14], rest[14:]
    x, core = lax.axis_index("x"), lax.axis_index("core")
    across = lax.rem(x + 2, NX)
    beside = x + 1 - 2 * lax.rem(x, 2)
    half = BLOCK_LEN // 2
    pairs = []
    for swap, unit in ((0, core), (1, 1 - core)):
        for source, (place, offset, length) in zip(
            inputs[7 * swap : 7 * swap + 7],
            (
                (x, 0, BLOCK_LEN),
                (beside, half, half),
                (NX - 1 - x, 0, half),
                (beside, 0, half),
                (NX - 1 - x, half, half),
                (across, 0, half),
                (across, half, half),
            ),
            strict=True,
        ):
            start = pl.multiple_of((NCORE * place + unit) * BLOCK_LEN + offset, half)
            pairs.append((source, held_ref.at[pl.ds(start, length)]))
    copies = fetch([(got_in, got_ref), (lag_in, lag_ref), *pairs], done)
    copies[0].wait()
    rows_ref[...] = got_ref[...].astype(f32).reshape(32 * 96, 128)
    left = []
    for a in range(NA):
        tiles = []
        for kind in range(3):
            for y in range(NY):
                for j in range(2):
                    lane = kind * 4 + j * 2
                    tiles.append(
                        jnp.concatenate(
                            [
                                rows_ref[pl.ds(y * 96 + (lane + half) * 8 + a, 8, stride=384), :]
                                for half in range(2)
                            ],
                            axis=1,
                        )
                    )
        left.append(jnp.concatenate(tiles, axis=0).astype(bf16))
    left = jnp.concatenate(left, axis=1)
    for copy in copies[1:]:
        copy.wait()
    total = product(left, held_ref[...], ((1,), (0,)))
    for lane in range(8):
        sums_ref[pl.ds(lane, 192, stride=8), :] = total[:, 128 * lane : 128 * lane + 128]
    out_ref[...] = jnp.concatenate(
        [sums_ref[...].reshape(BLOCKS, 24, 128), lag_ref[...]], axis=1
    ).astype(bf16)


def finish_kernel(got_ref, proj_ref, filter_ref, sums_ref, rows_ref):
    wide = got_ref[...].astype(f32)
    sums_ref[...] = (
        wide.reshape(NZ, NA, 32, 128)[:, :, :24, :].sum(axis=0).reshape(NA * 24, 128)
    )
    for e in range(3):
        for lane in range(8):
            proj_ref[8 * e : 8 * e + 8, 128 * lane : 128 * lane + 128] = sums_ref[
                pl.ds(8 * e + lane, 8, stride=24), :
            ]
    rows_ref[...] = wide.reshape(BLOCKS * 32, 128)
    for half in range(2):
        tiles = []
        for j in range(2):
            for z in range(NZ):
                start = z * 256 + 24 + 2 * j + half
                tiles.append(
                    rows_ref[pl.ds(start, 8, stride=32), :]
                    + rows_ref[pl.ds(start + 4, 8, stride=32), :]
                )
        filter_ref[128 * half : 128 * half + 128, :] = jnp.concatenate(tiles, axis=0).T


VMEM, HBM = pltpu.VMEM, pltpu.HBM


def call(kernel, name, args, spaces, outs, scratch, grant):
    return pl.pallas_call(
        kernel,
        out_shape=outs,
        in_specs=[pl.BlockSpec(memory_space=space) for space in spaces],
        out_specs=jax.tree.map(lambda _: pl.BlockSpec(memory_space=VMEM), outs),
        scratch_shapes=scratch,
        compiler_params=pltpu.CompilerParams(vmem_limit_bytes=grant * 2**20),
        name=name,
    )(*args)


def held_like(arrays):
    return [VMEM(array.shape, array.dtype) for array in arrays] + [
        pltpu.SemaphoreType.DMA((len(arrays),))
    ]


def on_device(layer_input, query_gate, key_gate, value_field, out_grad, filter_taps):
    pairs, rings = [(0, 1), (1, 0), (2, 3), (3, 2)], [(0, 3), (3, 0), (1, 2), (2, 1)]
    half = BLOCK_LEN // 2
    near_low = lax.ppermute(layer_input[half:], "x", pairs)
    far_high = lax.ppermute(layer_input[:half], "x", rings)
    sources = (key_gate, value_field, out_grad, query_gate, filter_taps, jnp.asarray(pack_order()))
    packed = call(
        pack_kernel,
        "pack",
        sources,
        [HBM] * 6,
        jax.ShapeDtypeStruct((BLOCKS, 24, 128), bf16),
        held_like(sources),
        60,
    )
    fields = lax.all_to_all(packed, ("z", "x", "core"), split_axis=0, concat_axis=0, tiled=True)
    grads, lags = call(
        conv_kernel,
        "conv",
        (fields, jnp.asarray(tables())),
        [VMEM] * 2,
        (
            jax.ShapeDtypeStruct((NZ * NY, 96, 128), bf16),
            jax.ShapeDtypeStruct((BLOCKS, 8, 128), f32),
        ),
        [VMEM((BLOCKS * 24, 128), f32), VMEM((BLOCKS * 8, 128), f32)],
        32,
    )
    grads, held, near_low, far_high = lax.optimization_barrier(
        (grads, layer_input, near_low, far_high)
    )
    near_high = lax.ppermute(held[:half], "x", pairs)
    far_low = lax.ppermute(held[half:], "x", rings)
    across_high = lax.ppermute(far_high, "x", pairs)
    across_low = lax.ppermute(near_low, "x", rings)
    own = (layer_input, near_low, far_high, near_high, far_low, across_high, across_low)
    other = [lax.ppermute(block, "core", [(0, 1), (1, 0)]) for block in own]
    stacked = lax.all_to_all(grads, ("z", "y"), split_axis=0, concat_axis=0, tiled=True)
    shares = call(
        share_kernel,
        "share",
        (stacked, lags, *own, *other),
        [pl.ANY] * 16,
        jax.ShapeDtypeStruct((BLOCKS, 32, 128), bf16),
        [
            VMEM((32, 96, 128), bf16),
            VMEM((BLOCKS, 8, 128), f32),
            VMEM((32 * 96, 128), f32),
            VMEM((2048, 1024), bf16),
            VMEM((1536, 128), f32),
            pltpu.SemaphoreType.DMA((16,)),
        ],
        52,
    )
    parts = lax.all_to_all(shares, ("z", "x", "core"), split_axis=0, concat_axis=0, tiled=True)
    return call(
        finish_kernel,
        "finish",
        (parts,),
        [VMEM],
        (
            jax.ShapeDtypeStruct((24, 1024), f32),
            jax.ShapeDtypeStruct((BLOCK_LEN, SHARD_CH), f32),
        ),
        [VMEM((NA * 24, 128), f32), VMEM((BLOCKS * 32, 128), f32)],
        32,
    )


def solution(mesh):
    fine = Mesh(mesh.devices.reshape(NZ, NX, NCORE, NY), ("z", "x", "core", "y"))
    spec = P(("z", "x", "core"), "y")
    return jax.shard_map(
        on_device,
        mesh=fine,
        in_specs=(spec,) * 6,
        out_specs=(spec, spec),
        check_vma=False,
    )
```

```python
import jax
import jax.numpy as jnp
import numpy as np
from jax import lax
from jax.experimental import pallas as pl
from jax.experimental.pallas import tpu as pltpu
from jax.sharding import Mesh
from jax.sharding import PartitionSpec as P

NZ, NX, NCORE, NA, NY = 8, 4, 2, 8, 4
BLOCKS, BLOCK_LEN, SHARD_CH = 64, 256, 128
BINS, TRANSFORM = 64, 32768
bf16, f32 = jnp.bfloat16, jnp.float32


def split_np(table):
    high = table.astype(np.float32).astype(jnp.bfloat16)
    low = (table - high.astype(np.float64)).astype(jnp.bfloat16)
    return high, low


def pack_order():
    rows = lax.broadcasted_iota(jnp.int32, (8 * BLOCKS, 4 * SHARD_CH), 0)
    columns = lax.broadcasted_iota(jnp.int32, (8 * BLOCKS, 4 * SHARD_CH), 1)
    s, j, half = (rows >> 2) & 1, (rows >> 1) & 1, rows & 1
    wanted = ((2 * s + half) << 7) + (j << 6) + (rows >> 3)
    return jnp.where(columns == wanted, 1.0, 0.0).astype(bf16)


def tables():
    bins = np.arange(BINS, dtype=np.float64) + 0.5
    held = np.arange(BLOCKS, dtype=np.float64)
    lag = np.arange(BLOCK_LEN, dtype=np.float64)
    first = 2.0 * np.pi / 128.0 * bins[:, None] * held[None, :]
    twist = 2.0 * np.pi / TRANSFORM * bins[:, None] * lag[None, :]
    second = 2.0 * np.pi / BLOCK_LEN * ((lag[:, None] * lag[None, :]) % BLOCK_LEN)
    ahead_high, ahead_low = split_np(np.concatenate([np.cos(first), -np.sin(first)], axis=0))
    back = np.concatenate([np.cos(first).T, -np.sin(first).T], axis=1) * (2.0 / TRANSFORM)
    back_high, back_low = split_np(back)
    cosine, sine = np.cos(second), np.sin(second)
    outer = split_np(np.block([[cosine, -sine], [sine, cosine]]))
    turn = split_np(np.concatenate([np.cos(twist), -np.sin(twist)], axis=1))
    ahead = np.concatenate([ahead_high, ahead_high, ahead_low], axis=1)
    back = np.concatenate([back_high, back_high, back_low], axis=1)
    ahead = np.pad(ahead, ((0, 0), (0, 512 - ahead.shape[1])))
    back = np.pad(back, ((0, 0), (0, 512 - back.shape[1])))
    return np.concatenate([*outer, *turn, ahead, back], axis=0)


def split(value):
    high = value.astype(bf16)
    low = (value - high.astype(f32)).astype(bf16)
    return high, low


def product(left, right, dims):
    return lax.dot_general(left, right, (dims, ((), ())), preferred_element_type=f32)


def fetch(pairs, done):
    copies = [
        pltpu.make_async_copy(source, target, done.at[number])
        for number, (source, target) in enumerate(pairs)
    ]
    for copy in copies:
        copy.start()
    return copies


def pack_kernel(key_in, value_in, grad_in, query_in, taps_in, out_ref, *scratch):
    *held, done = scratch
    key_ref, value_ref, grad_ref, query_ref, taps_ref = held
    sources = (key_in, value_in, grad_in, query_in, taps_in)
    copies = fetch(zip(sources, held, strict=True), done)
    order = pack_order()
    for copy in copies:
        copy.wait()
    taps_high, taps_low = split(taps_ref[...])

    def tile(first, second):
        wide = jnp.concatenate(
            [first[:128], first[128:], second[:128], second[128:]], axis=1
        )
        return product(order, wide, ((1,), (1,))).reshape(BLOCKS, 8, 128)

    out_ref[...] = jnp.concatenate(
        [
            tile(key_ref[...], value_ref[...]),
            tile(grad_ref[...], query_ref[...]),
            tile(taps_high, taps_low),
        ],
        axis=1,
    ).astype(bf16)


def conv_kernel(got_ref, table_ref, out_ref, lag_ref, rows_ref, lag_rows_ref):
    rows_ref[...] = got_ref[...].astype(f32).reshape(BLOCKS * 24, 128)

    def field(number):
        parts = []
        for z in range(NZ):
            parts.append(
                jnp.concatenate(
                    [rows_ref[pl.ds(z * 192 + number * 4 + r, 8, stride=24), :] for r in range(4)],
                    axis=1,
                )
            )
        return jnp.concatenate(parts, axis=0)

    key, value, grad, query = field(0), field(1), field(2), field(3)
    taps = field(4) + field(5)
    signals = jnp.concatenate([taps, key * value, grad * query], axis=1)
    sig_high, sig_low = split(signals)
    mixed = product(
        table_ref[1152:1280, :192], jnp.concatenate([sig_high, sig_low, sig_high], axis=0), ((1,), (0,))
    )
    turn = table_ref[1024:1088].astype(f32) + table_ref[1088:1152].astype(f32)
    turn_real, turn_imag = turn[:, :256], turn[:, 256:]
    turned = []
    for block in range(6):
        real = mixed[:BINS, 256 * block : 256 * (block + 1)]
        imag = mixed[BINS:, 256 * block : 256 * (block + 1)]
        turned.append(
            jnp.concatenate(
                [real * turn_real - imag * turn_imag, real * turn_imag + imag * turn_real], axis=1
            )
        )
    outer_high, outer_low = table_ref[:512], table_ref[512:1024]

    def outer(source, dims):
        high, low = split(source)
        return (
            product(high, outer_high, dims)
            + product(low, outer_high, dims)
            + product(high, outer_low, dims)
        )

    spec = outer(jnp.concatenate(turned, axis=0), ((1,), (0,)))
    tr, ti = spec[:128, :256], spec[:128, 256:]
    vr, vi = spec[128:256, :256], spec[128:256, 256:]
    ur, ui = spec[256:, :256], spec[256:, 256:]
    mixes = jnp.concatenate(
        [
            jnp.concatenate([tr * vr - ti * vi, tr * vi + ti * vr], axis=1),
            jnp.concatenate([tr * ur + ti * ui, tr * ui - ti * ur], axis=1),
            jnp.concatenate([vr * ur + vi * ui, vr * ui - vi * ur], axis=1),
        ],
        axis=0,
    )
    home = outer(mixes, ((1,), (1,)))
    reals, imags = [], []
    for block in range(6):
        real = home[BINS * block : BINS * (block + 1), :256]
        imag = home[BINS * block : BINS * (block + 1), 256:]
        reals.append(real * turn_real + imag * turn_imag)
        imags.append(imag * turn_real - real * turn_imag)
    untwisted = jnp.concatenate(
        [jnp.concatenate(reals, axis=1), jnp.concatenate(imags, axis=1)], axis=0
    )
    home_high, home_low = split(untwisted)
    result = product(
        table_ref[1280:1344, :384], jnp.concatenate([home_high, home_low, home_high], axis=0), ((1,), (0,))
    )
    conv_out, gated_grad, lag_grad = result[:, :512], result[:, 512:1024], result[:, 1024:]
    stacked = (grad * conv_out, gated_grad * value, gated_grad * key)
    for z in range(NZ):
        block = jnp.concatenate(
            [
                field_rows[8 * z : 8 * z + 8, 128 * lane : 128 * lane + 128]
                for field_rows in stacked
                for lane in range(4)
            ],
            axis=0,
        ).astype(bf16)
        for y in range(NY):
            out_ref[z * NY + y] = block
    lag_high = lag_grad.astype(bf16).astype(f32)
    lag_low = lag_grad - lag_high
    for level, part in ((0, lag_high), (1, lag_low)):
        for z in range(NZ):
            for r in range(4):
                lag_rows_ref[pl.ds(z * 64 + 4 * level + r, 8, stride=8), :] = part[
                    8 * z : 8 * z + 8, 128 * r : 128 * r + 128
                ]
    lag_ref[...] = lag_rows_ref[...].reshape(BLOCKS, 8, 128)


def share_kernel(got_in, lag_in, *rest):
    inputs, (out_ref, got_ref, lag_ref, rows_ref, held_ref, sums_ref, done) = rest[:14], rest[14:]
    x, core = lax.axis_index("x"), lax.axis_index("core")
    across = lax.rem(x + 2, NX)
    beside = x + 1 - 2 * lax.rem(x, 2)
    half = BLOCK_LEN // 2
    pairs = []
    for swap, unit in ((0, core), (1, 1 - core)):
        for source, (place, offset, length) in zip(
            inputs[7 * swap : 7 * swap + 7],
            (
                (x, 0, BLOCK_LEN),
                (beside, half, half),
                (NX - 1 - x, 0, half),
                (beside, 0, half),
                (NX - 1 - x, half, half),
                (across, 0, half),
                (across, half, half),
            ),
            strict=True,
        ):
            start = pl.multiple_of((NCORE * place + unit) * BLOCK_LEN + offset, half)
            pairs.append((source, held_ref.at[pl.ds(start, length)]))
    copies = fetch([(got_in, got_ref), (lag_in, lag_ref), *pairs], done)
    copies[0].wait()
    rows_ref[...] = got_ref[...].astype(f32).reshape(32 * 96, 128)
    left = []
    for a in range(NA):
        tiles = []
        for kind in range(3):
            for y in range(NY):
                for j in range(2):
                    lane = kind * 4 + j * 2
                    tiles.append(
                        jnp.concatenate(
                            [
                                rows_ref[pl.ds(y * 96 + (lane + half) * 8 + a, 8, stride=384), :]
                                for half in range(2)
                            ],
                            axis=1,
                        )
                    )
        left.append(jnp.concatenate(tiles, axis=0).astype(bf16))
    left = jnp.concatenate(left, axis=1)
    for copy in copies[1:]:
        copy.wait()
    total = product(left, held_ref[...], ((1,), (0,)))
    for lane in range(8):
        sums_ref[pl.ds(lane, 192, stride=8), :] = total[:, 128 * lane : 128 * lane + 128]
    out_ref[...] = jnp.concatenate(
        [sums_ref[...].reshape(BLOCKS, 24, 128), lag_ref[...]], axis=1
    ).astype(bf16)


def finish_kernel(got_ref, proj_ref, filter_ref, sums_ref, rows_ref):
    wide = got_ref[...].astype(f32)
    sums_ref[...] = (
        wide.reshape(NZ, NA, 32, 128)[:, :, :24, :].sum(axis=0).reshape(NA * 24, 128)
    )
    for e in range(3):
        for lane in range(8):
            proj_ref[8 * e : 8 * e + 8, 128 * lane : 128 * lane + 128] = sums_ref[
                pl.ds(8 * e + lane, 8, stride=24), :
            ]
    rows_ref[...] = wide.reshape(BLOCKS * 32, 128)
    for half in range(2):
        tiles = []
        for j in range(2):
            for z in range(NZ):
                start = z * 256 + 24 + 2 * j + half
                tiles.append(
                    rows_ref[pl.ds(start, 8, stride=32), :]
                    + rows_ref[pl.ds(start + 4, 8, stride=32), :]
                )
        filter_ref[128 * half : 128 * half + 128, :] = jnp.concatenate(tiles, axis=0).T


VMEM, HBM = pltpu.VMEM, pltpu.HBM


def call(kernel, name, args, spaces, outs, scratch, grant):
    return pl.pallas_call(
        kernel,
        out_shape=outs,
        in_specs=[pl.BlockSpec(memory_space=space) for space in spaces],
        out_specs=jax.tree.map(lambda _: pl.BlockSpec(memory_space=VMEM), outs),
        scratch_shapes=scratch,
        compiler_params=pltpu.CompilerParams(vmem_limit_bytes=grant * 2**20),
        name=name,
    )(*args)


def held_like(arrays):
    return [VMEM(array.shape, array.dtype) for array in arrays] + [
        pltpu.SemaphoreType.DMA((len(arrays),))
    ]


def on_device(layer_input, query_gate, key_gate, value_field, out_grad, filter_taps):
    pairs, rings = [(0, 1), (1, 0), (2, 3), (3, 2)], [(0, 3), (3, 0), (1, 2), (2, 1)]
    half = BLOCK_LEN // 2
    near_low = lax.ppermute(layer_input[half:], "x", pairs)
    far_high = lax.ppermute(layer_input[:half], "x", rings)
    sources = (key_gate, value_field, out_grad, query_gate, filter_taps)
    packed = call(
        pack_kernel,
        "pack",
        sources,
        [HBM] * 5,
        jax.ShapeDtypeStruct((BLOCKS, 24, 128), bf16),
        held_like(sources),
        60,
    )
    fields = lax.all_to_all(packed, ("z", "x", "core"), split_axis=0, concat_axis=0, tiled=True)
    grads, lags = call(
        conv_kernel,
        "conv",
        (fields, jnp.asarray(tables())),
        [VMEM] * 2,
        (
            jax.ShapeDtypeStruct((NZ * NY, 96, 128), bf16),
            jax.ShapeDtypeStruct((BLOCKS, 8, 128), f32),
        ),
        [VMEM((BLOCKS * 24, 128), f32), VMEM((BLOCKS * 8, 128), f32)],
        32,
    )
    grads, held, near_low, far_high = lax.optimization_barrier(
        (grads, layer_input, near_low, far_high)
    )
    near_high = lax.ppermute(held[:half], "x", pairs)
    far_low = lax.ppermute(held[half:], "x", rings)
    across_high = lax.ppermute(far_high, "x", pairs)
    across_low = lax.ppermute(near_low, "x", rings)
    own = (layer_input, near_low, far_high, near_high, far_low, across_high, across_low)
    other = [lax.ppermute(block, "core", [(0, 1), (1, 0)]) for block in own]
    stacked = lax.all_to_all(grads, ("z", "y"), split_axis=0, concat_axis=0, tiled=True)
    shares = call(
        share_kernel,
        "share",
        (stacked, lags, *own, *other),
        [pl.ANY] * 16,
        jax.ShapeDtypeStruct((BLOCKS, 32, 128), bf16),
        [
            VMEM((32, 96, 128), bf16),
            VMEM((BLOCKS, 8, 128), f32),
            VMEM((32 * 96, 128), f32),
            VMEM((2048, 1024), bf16),
            VMEM((1536, 128), f32),
            pltpu.SemaphoreType.DMA((16,)),
        ],
        52,
    )
    parts = lax.all_to_all(shares, ("z", "x", "core"), split_axis=0, concat_axis=0, tiled=True)
    return call(
        finish_kernel,
        "finish",
        (parts,),
        [VMEM],
        (
            jax.ShapeDtypeStruct((24, 1024), f32),
            jax.ShapeDtypeStruct((BLOCK_LEN, SHARD_CH), f32),
        ),
        [VMEM((NA * 24, 128), f32), VMEM((BLOCKS * 32, 128), f32)],
        32,
    )


def solution(mesh):
    fine = Mesh(mesh.devices.reshape(NZ, NX, NCORE, NY), ("z", "x", "core", "y"))
    spec = P(("z", "x", "core"), "y")
    return jax.shard_map(
        on_device,
        mesh=fine,
        in_specs=(spec,) * 6,
        out_specs=(spec, spec),
        check_vma=False,
    )
```

```python
import jax
import jax.numpy as jnp
import numpy as np
from jax import lax
from jax.experimental import pallas as pl
from jax.experimental.pallas import tpu as pltpu
from jax.sharding import Mesh
from jax.sharding import PartitionSpec as P

NZ, NX, NCORE, NA, NY = 8, 4, 2, 8, 4
BLOCKS, BLOCK_LEN, SHARD_CH = 64, 256, 128
BINS, TRANSFORM = 64, 32768
bf16, f32 = jnp.bfloat16, jnp.float32


def split_np(table):
    high = table.astype(np.float32).astype(jnp.bfloat16)
    low = (table - high.astype(np.float64)).astype(jnp.bfloat16)
    return high, low


def pack_order():
    rows = lax.broadcasted_iota(jnp.int32, (8 * BLOCKS, 4 * SHARD_CH), 0)
    columns = lax.broadcasted_iota(jnp.int32, (8 * BLOCKS, 4 * SHARD_CH), 1)
    s, j, half = (rows >> 2) & 1, (rows >> 1) & 1, rows & 1
    wanted = ((2 * s + half) << 7) + (j << 6) + (rows >> 3)
    return jnp.where(columns == wanted, 1.0, 0.0).astype(bf16)


def tables():
    bins = np.arange(BINS, dtype=np.float64) + 0.5
    held = np.arange(BLOCKS, dtype=np.float64)
    lag = np.arange(BLOCK_LEN, dtype=np.float64)
    first = 2.0 * np.pi / 128.0 * bins[:, None] * held[None, :]
    twist = 2.0 * np.pi / TRANSFORM * bins[:, None] * lag[None, :]
    second = 2.0 * np.pi / BLOCK_LEN * ((lag[:, None] * lag[None, :]) % BLOCK_LEN)
    ahead_high, ahead_low = split_np(np.concatenate([np.cos(first), -np.sin(first)], axis=0))
    back = np.concatenate([np.cos(first).T, -np.sin(first).T], axis=1) * (2.0 / TRANSFORM)
    back_high, back_low = split_np(back)
    cosine, sine = np.cos(second), np.sin(second)
    outer = split_np(np.block([[cosine, -sine], [sine, cosine]]))
    turn = split_np(np.concatenate([np.cos(twist), -np.sin(twist)], axis=1))
    ahead = np.concatenate([ahead_high, ahead_high, ahead_low], axis=1)
    back = np.concatenate([back_high, back_high, back_low], axis=1)
    ahead = np.pad(ahead, ((0, 0), (0, 512 - ahead.shape[1])))
    back = np.pad(back, ((0, 0), (0, 512 - back.shape[1])))
    return np.concatenate([*outer, *turn, ahead, back], axis=0)


def split(value):
    high = value.astype(bf16)
    low = (value - high.astype(f32)).astype(bf16)
    return high, low


def product(left, right, dims):
    return lax.dot_general(left, right, (dims, ((), ())), preferred_element_type=f32)


def fetch(pairs, done):
    copies = [
        pltpu.make_async_copy(source, target, done.at[number])
        for number, (source, target) in enumerate(pairs)
    ]
    for copy in copies:
        copy.start()
    return copies


def pack_kernel(key_in, value_in, grad_in, query_in, taps_in, out_ref, *scratch):
    *held, done, packed_ref, left = scratch
    key_ref, value_ref, grad_ref, query_ref, taps_ref = held
    sources = (key_in, value_in, grad_in, query_in, taps_in)
    copies = fetch(zip(sources, held, strict=True), done)
    order = pack_order()
    for copy in copies:
        copy.wait()
    taps_high, taps_low = split(taps_ref[...])

    def wide(first, second):
        return jnp.concatenate([first[:128], first[128:], second[:128], second[128:]], axis=1)

    fields = (
        wide(key_ref[...], value_ref[...]),
        wide(grad_ref[...], query_ref[...]),
        wide(taps_high, taps_low),
    )
    leaving = []
    for part in range(2):
        rows = order[256 * part : 256 * part + 256]
        tiles = [product(rows, field, ((1,), (1,))).reshape(32, 8, 128) for field in fields]
        blocks = pl.ds(32 * part, 32)
        packed_ref[blocks] = jnp.concatenate(tiles, axis=1).astype(bf16)
        copy = pltpu.make_async_copy(packed_ref.at[blocks], out_ref.at[blocks], left.at[part])
        copy.start()
        leaving.append(copy)
    for copy in leaving:
        copy.wait()


def conv_kernel(got_ref, table_ref, out_ref, lag_ref, rows_ref, lag_rows_ref):
    rows_ref[...] = got_ref[...].astype(f32).reshape(BLOCKS * 24, 128)

    def field(number):
        parts = []
        for z in range(NZ):
            parts.append(
                jnp.concatenate(
                    [rows_ref[pl.ds(z * 192 + number * 4 + r, 8, stride=24), :] for r in range(4)],
                    axis=1,
                )
            )
        return jnp.concatenate(parts, axis=0)

    key, value, grad, query = field(0), field(1), field(2), field(3)
    taps = field(4) + field(5)
    signals = jnp.concatenate([taps, key * value, grad * query], axis=1)
    sig_high, sig_low = split(signals)
    mixed = product(
        table_ref[1152:1280, :192], jnp.concatenate([sig_high, sig_low, sig_high], axis=0), ((1,), (0,))
    )
    turn = table_ref[1024:1088].astype(f32) + table_ref[1088:1152].astype(f32)
    turn_real, turn_imag = turn[:, :256], turn[:, 256:]
    turned = []
    for block in range(6):
        real = mixed[:BINS, 256 * block : 256 * (block + 1)]
        imag = mixed[BINS:, 256 * block : 256 * (block + 1)]
        turned.append(
            jnp.concatenate(
                [real * turn_real - imag * turn_imag, real * turn_imag + imag * turn_real], axis=1
            )
        )
    outer_high, outer_low = table_ref[:512], table_ref[512:1024]

    def outer(source, dims):
        high, low = split(source)
        return (
            product(high, outer_high, dims)
            + product(low, outer_high, dims)
            + product(high, outer_low, dims)
        )

    spec = outer(jnp.concatenate(turned, axis=0), ((1,), (0,)))
    tr, ti = spec[:128, :256], spec[:128, 256:]
    vr, vi = spec[128:256, :256], spec[128:256, 256:]
    ur, ui = spec[256:, :256], spec[256:, 256:]
    mixes = jnp.concatenate(
        [
            jnp.concatenate([tr * vr - ti * vi, tr * vi + ti * vr], axis=1),
            jnp.concatenate([tr * ur + ti * ui, tr * ui - ti * ur], axis=1),
            jnp.concatenate([vr * ur + vi * ui, vr * ui - vi * ur], axis=1),
        ],
        axis=0,
    )
    home = outer(mixes, ((1,), (1,)))
    reals, imags = [], []
    for block in range(6):
        real = home[BINS * block : BINS * (block + 1), :256]
        imag = home[BINS * block : BINS * (block + 1), 256:]
        reals.append(real * turn_real + imag * turn_imag)
        imags.append(imag * turn_real - real * turn_imag)
    untwisted = jnp.concatenate(
        [jnp.concatenate(reals, axis=1), jnp.concatenate(imags, axis=1)], axis=0
    )
    home_high, home_low = split(untwisted)
    result = product(
        table_ref[1280:1344, :384], jnp.concatenate([home_high, home_low, home_high], axis=0), ((1,), (0,))
    )
    conv_out, gated_grad, lag_grad = result[:, :512], result[:, 512:1024], result[:, 1024:]
    stacked = (grad * conv_out, gated_grad * value, gated_grad * key)
    for z in range(NZ):
        block = jnp.concatenate(
            [
                field_rows[8 * z : 8 * z + 8, 128 * lane : 128 * lane + 128]
                for field_rows in stacked
                for lane in range(4)
            ],
            axis=0,
        ).astype(bf16)
        for y in range(NY):
            out_ref[z * NY + y] = block
    lag_high = lag_grad.astype(bf16).astype(f32)
    lag_low = lag_grad - lag_high
    for level, part in ((0, lag_high), (1, lag_low)):
        for z in range(NZ):
            for r in range(4):
                lag_rows_ref[pl.ds(z * 64 + 4 * level + r, 8, stride=8), :] = part[
                    8 * z : 8 * z + 8, 128 * r : 128 * r + 128
                ]
    lag_ref[...] = lag_rows_ref[...].reshape(BLOCKS, 8, 128)


def share_kernel(got_in, lag_in, *rest):
    inputs, (out_ref, got_ref, lag_ref, rows_ref, held_ref, sums_ref, done) = rest[:14], rest[14:]
    x, core = lax.axis_index("x"), lax.axis_index("core")
    across = lax.rem(x + 2, NX)
    beside = x + 1 - 2 * lax.rem(x, 2)
    half = BLOCK_LEN // 2
    pairs = []
    for swap, unit in ((0, core), (1, 1 - core)):
        for source, (place, offset, length) in zip(
            inputs[7 * swap : 7 * swap + 7],
            (
                (x, 0, BLOCK_LEN),
                (beside, half, half),
                (NX - 1 - x, 0, half),
                (beside, 0, half),
                (NX - 1 - x, half, half),
                (across, 0, half),
                (across, half, half),
            ),
            strict=True,
        ):
            start = pl.multiple_of((NCORE * place + unit) * BLOCK_LEN + offset, half)
            pairs.append((source, held_ref.at[pl.ds(start, length)]))
    copies = fetch([(got_in, got_ref), (lag_in, lag_ref), *pairs], done)
    copies[0].wait()
    rows_ref[...] = got_ref[...].astype(f32).reshape(32 * 96, 128)
    left = []
    for a in range(NA):
        tiles = []
        for kind in range(3):
            for y in range(NY):
                for j in range(2):
                    lane = kind * 4 + j * 2
                    tiles.append(
                        jnp.concatenate(
                            [
                                rows_ref[pl.ds(y * 96 + (lane + half) * 8 + a, 8, stride=384), :]
                                for half in range(2)
                            ],
                            axis=1,
                        )
                    )
        left.append(jnp.concatenate(tiles, axis=0).astype(bf16))
    left = jnp.concatenate(left, axis=1)
    for copy in copies[1:]:
        copy.wait()
    total = product(left, held_ref[...], ((1,), (0,)))
    for lane in range(8):
        sums_ref[pl.ds(lane, 192, stride=8), :] = total[:, 128 * lane : 128 * lane + 128]
    out_ref[...] = jnp.concatenate(
        [sums_ref[...].reshape(BLOCKS, 24, 128), lag_ref[...]], axis=1
    ).astype(bf16)


def finish_kernel(got_ref, proj_ref, filter_ref, sums_ref, rows_ref):
    wide = got_ref[...].astype(f32)
    sums_ref[...] = (
        wide.reshape(NZ, NA, 32, 128)[:, :, :24, :].sum(axis=0).reshape(NA * 24, 128)
    )
    for e in range(3):
        for lane in range(8):
            proj_ref[8 * e : 8 * e + 8, 128 * lane : 128 * lane + 128] = sums_ref[
                pl.ds(8 * e + lane, 8, stride=24), :
            ]
    rows_ref[...] = wide.reshape(BLOCKS * 32, 128)
    for half in range(2):
        tiles = []
        for j in range(2):
            for z in range(NZ):
                start = z * 256 + 24 + 2 * j + half
                tiles.append(
                    rows_ref[pl.ds(start, 8, stride=32), :]
                    + rows_ref[pl.ds(start + 4, 8, stride=32), :]
                )
        filter_ref[128 * half : 128 * half + 128, :] = jnp.concatenate(tiles, axis=0).T


VMEM, HBM = pltpu.VMEM, pltpu.HBM


def call(kernel, name, args, spaces, outs, scratch, grant, places=VMEM):
    return pl.pallas_call(
        kernel,
        out_shape=outs,
        in_specs=[pl.BlockSpec(memory_space=space) for space in spaces],
        out_specs=jax.tree.map(lambda _: pl.BlockSpec(memory_space=places), outs),
        scratch_shapes=scratch,
        compiler_params=pltpu.CompilerParams(vmem_limit_bytes=grant * 2**20),
        name=name,
    )(*args)


def held_like(arrays):
    return [VMEM(array.shape, array.dtype) for array in arrays] + [
        pltpu.SemaphoreType.DMA((len(arrays),))
    ]


def on_device(layer_input, query_gate, key_gate, value_field, out_grad, filter_taps):
    pairs, rings = [(0, 1), (1, 0), (2, 3), (3, 2)], [(0, 3), (3, 0), (1, 2), (2, 1)]
    half = BLOCK_LEN // 2
    near_low = lax.ppermute(layer_input[half:], "x", pairs)
    far_high = lax.ppermute(layer_input[:half], "x", rings)
    sources = (key_gate, value_field, out_grad, query_gate, filter_taps)
    packed = call(
        pack_kernel,
        "pack",
        sources,
        [HBM] * 5,
        jax.ShapeDtypeStruct((BLOCKS, 24, 128), bf16),
        held_like(sources)
        + [VMEM((BLOCKS, 24, 128), bf16), pltpu.SemaphoreType.DMA((2,))],
        60,
        pl.ANY,
    )
    fields = lax.all_to_all(packed, ("z", "x", "core"), split_axis=0, concat_axis=0, tiled=True)
    grads, lags = call(
        conv_kernel,
        "conv",
        (fields, jnp.asarray(tables())),
        [VMEM] * 2,
        (
            jax.ShapeDtypeStruct((NZ * NY, 96, 128), bf16),
            jax.ShapeDtypeStruct((BLOCKS, 8, 128), f32),
        ),
        [VMEM((BLOCKS * 24, 128), f32), VMEM((BLOCKS * 8, 128), f32)],
        32,
    )
    grads, held, near_low, far_high = lax.optimization_barrier(
        (grads, layer_input, near_low, far_high)
    )
    near_high = lax.ppermute(held[:half], "x", pairs)
    far_low = lax.ppermute(held[half:], "x", rings)
    across_high = lax.ppermute(far_high, "x", pairs)
    across_low = lax.ppermute(near_low, "x", rings)
    own = (layer_input, near_low, far_high, near_high, far_low, across_high, across_low)
    other = [lax.ppermute(block, "core", [(0, 1), (1, 0)]) for block in own]
    stacked = lax.all_to_all(grads, ("z", "y"), split_axis=0, concat_axis=0, tiled=True)
    shares = call(
        share_kernel,
        "share",
        (stacked, lags, *own, *other),
        [pl.ANY] * 16,
        jax.ShapeDtypeStruct((BLOCKS, 32, 128), bf16),
        [
            VMEM((32, 96, 128), bf16),
            VMEM((BLOCKS, 8, 128), f32),
            VMEM((32 * 96, 128), f32),
            VMEM((2048, 1024), bf16),
            VMEM((1536, 128), f32),
            pltpu.SemaphoreType.DMA((16,)),
        ],
        52,
    )
    parts = lax.all_to_all(shares, ("z", "x", "core"), split_axis=0, concat_axis=0, tiled=True)
    return call(
        finish_kernel,
        "finish",
        (parts,),
        [VMEM],
        (
            jax.ShapeDtypeStruct((24, 1024), f32),
            jax.ShapeDtypeStruct((BLOCK_LEN, SHARD_CH), f32),
        ),
        [VMEM((NA * 24, 128), f32), VMEM((BLOCKS * 32, 128), f32)],
        32,
    )


def solution(mesh):
    fine = Mesh(mesh.devices.reshape(NZ, NX, NCORE, NY), ("z", "x", "core", "y"))
    spec = P(("z", "x", "core"), "y")
    return jax.shard_map(
        on_device,
        mesh=fine,
        in_specs=(spec,) * 6,
        out_specs=(spec, spec),
        check_vma=False,
    )
```
